32 devices in a mesh: term: 2 (over y), sector: 16 (over z, x, core).
Axes of the slice: x: 2, y: 2, z: 4, core: 2. Of those that a mesh axis runs over, the one named last changes fastest.
Arguments:
- psi: float32 [256, 128, 128], P('sector'), may hold values from -6 to 6
- left_env: float32 [8, 256, 128, 128], P('term', 'sector'), may hold values from -0.5 to 0.5
- right_env: float32 [8, 256, 128, 128], P('term', 'sector'), may hold values from -0.1875 to 0.1875
- target: int32 [8, 256], P('term', 'sector'), may hold values from 0 to 255, as said below
Outputs:
- sigma: float32 [256, 128, 128], P('sector', 'term')
The draws below stay inside these ranges and needn't reach their ends.
Inputs may be any that keep to these rules, and one draw needn't show every extreme that they name: Among the 4 * 16 pairs of terms w in one block of 4 consecutive terms and source blocks s in one block of 16 consecutive blocks, at most 4 have their target in any one block of 16 consecutive target blocks, and exactly 4 do for some such block.
All inputs are finite; a program needn't handle non-finite values.
Results may differ from the reference program's by a relative error of at most 0.0001.
Values sent between devices are 32-bit elements; how exact they have to be, the bound alone decides.
A program may use at most 128 MiB of HBM per device.

```python
import jax
import jax.numpy as jnp
from jax import lax

B = 128
K_DEV = 4
S_DEV = 16
CAP = 4
K = 8
NS = 256
N_TERM = 2
N_SECTOR = 16


def draw_target(key, part):
    item_count = K_DEV * S_DEV
    device_keys = jax.random.split(key, N_TERM * N_SECTOR)

    def one_block(sub):
        key_one, key_two, key_three, key_four = jax.random.split(sub, 4)
        chosen = jax.random.randint(key_one, (), 0, N_SECTOR)
        others = jax.random.permutation(key_two, (N_SECTOR - 1) * CAP)[:item_count - CAP]
        others = jnp.where(others >= CAP * chosen, others + CAP, others)
        slots_all = jnp.concatenate([chosen * CAP + jnp.arange(CAP), others])
        slots_all = jax.random.permutation(key_three, slots_all)
        local_pick = jax.random.randint(key_four, (item_count,), 0, S_DEV)
        return slots_all // CAP * S_DEV + local_pick
    values = jax.vmap(one_block)(device_keys)
    values = values.reshape(N_TERM, N_SECTOR, K_DEV, S_DEV).transpose(0, 2, 1, 3)
    return values.reshape(K_DEV * N_TERM, S_DEV * N_SECTOR).astype(jnp.int32)


def shard_levels(own_key, shape, cuts, smallest, high):
    gain = 1.0
    for dim, blocks in cuts:
        draws = jax.random.uniform(jax.random.fold_in(jax.random.fold_in(own_key, 6), dim), (blocks,), jnp.float32, smallest / len(cuts), high / len(cuts))
        gain = gain * jnp.repeat(jnp.exp(draws), shape[dim] // blocks).reshape((-1,) + (1,) * (len(shape) - 1 - dim))
    return gain


def centred(rng, dims, width, limit, cuts=(), held_as=jnp.bfloat16):
    level = shard_levels(rng, dims, cuts, -0.22, 0.18) if cuts else 1.0
    entries = jax.random.normal(rng, dims, jnp.float32) * width * level
    return jnp.minimum(jnp.maximum(entries, -limit), limit).astype(held_as)


def setup_inputs(seed: int = 0) -> dict:
    streams_of = jax.random.split(jax.random.key(seed), 5)
    psi = centred(streams_of[0], (NS, B, B), 1.0, 6.0, ((0, 16),), jnp.float32)
    left_env = centred(streams_of[1], (K, NS, B, B), B ** -0.5, 0.5, ((0, 2), (1, 16)), jnp.float32)
    right_env = centred(streams_of[2], (K, NS, B, B), (B * K) ** -0.5, 0.1875, ((0, 2), (1, 16)), jnp.float32)
    target = draw_target(jax.random.fold_in(streams_of[4], 71), 0)
    return {"psi": psi, "left_env": left_env, "right_env": right_env, "target": target}


def reference(psi, left_env, right_env, target):
    def one_term(carry, inputs):
        left_w, right_w, target_w = inputs
        contracted = jnp.einsum('sab,sbc->sac', left_w, psi, precision=lax.Precision.HIGHEST)
        picked = right_w[target_w]
        products = jnp.einsum('sab,sbc->sac', contracted, picked, precision=lax.Precision.HIGHEST)
        summed = jax.ops.segment_sum(products, target_w, num_segments=psi.shape[0])
        return carry + summed, None

    total, unused = lax.scan(one_term, jnp.zeros(psi.shape, jnp.float32), (left_env, right_env, target))
    return total
```

```python
import functools

import jax
import jax.numpy as jnp
from jax import lax
from jax.experimental import pallas as pl
from jax.experimental.pallas import tpu as pltpu
from jax.sharding import PartitionSpec as P

CAP = 4
CHUNKS = 2
MESH = pl.DeviceIdType.MESH


def shifted(me, step, sign, count):
    high = count // 4
    d_high, d_mid, d_low = step // 4, (step // 2) % 2, step % 2
    z, x, c = me // 4, (me // 2) % 2, me % 2
    z = lax.rem(z + (d_high if sign > 0 else high - d_high), high)
    x = lax.rem(x + d_mid, 2)
    c = lax.rem(c + d_low, 2)
    return (z * 2 + x) * 2 + c


def kernel(
    n_sector, n_term, target, psi_hbm, left_hbm, right_hbm, out,
    psi, left, right, send, recv, partial, from_term,
    labels, held_items, held_labels,
    load_sem, label_send, label_recv, data_send, data_recv, term_send, term_recv,
):
    terms, blocks = target.shape
    width = psi.shape[-1]
    rows = width // n_term
    part = rows // CHUNKS
    me = lax.axis_index("sector")
    my_term = lax.axis_index("term")

    load_psi = pltpu.make_async_copy(psi_hbm, psi, load_sem.at[0])
    load_left = pltpu.make_async_copy(left_hbm, left, load_sem.at[1])
    load_right = pltpu.make_async_copy(right_hbm, right, load_sem.at[2])
    load_psi.start()
    load_left.start()
    load_right.start()

    barrier = pltpu.get_barrier_semaphore()

    def greet(step, carry):
        peer = shifted(me, step, 1, n_sector)
        pl.semaphore_signal(barrier, inc=1, device_id={"sector": peer}, device_id_type=MESH)
        return carry

    lax.fori_loop(1, n_sector, greet, 0)
    for other in range(1, n_term):
        pl.semaphore_signal(
            barrier, inc=1, device_id={"term": lax.rem(my_term + other, n_term)}, device_id_type=MESH
        )
    pl.semaphore_wait(barrier, n_sector + n_term - 2)

    def label_copy(step):
        return pltpu.make_async_remote_copy(
            src_ref=target,
            dst_ref=labels.at[step],
            send_sem=label_send.at[step],
            recv_sem=label_recv.at[step],
            device_id={"sector": shifted(me, step, 1, n_sector)},
            device_id_type=MESH,
        )

    def data_copy(chunk, step):
        return pltpu.make_async_remote_copy(
            src_ref=send.at[chunk, step],
            dst_ref=recv.at[chunk, step],
            send_sem=data_send.at[chunk, step],
            recv_sem=data_recv.at[chunk, step],
            device_id={"sector": shifted(me, step, 1, n_sector)},
            device_id_type=MESH,
        )

    def find(read, owner):
        low = owner * blocks

        def scan(item, carry):
            count, found = carry
            local = read(item // blocks, item % blocks) - low
            hit = (local >= 0) & (local < blocks)
            code = item * blocks + local
            found = tuple(
                jnp.where(hit & (count == slot), code, had) for slot, had in enumerate(found)
            )
            return count + hit.astype(jnp.int32), found

        _, found = lax.fori_loop(
            0, terms * blocks, scan, (jnp.int32(0), (jnp.int32(-1),) * CAP), unroll=4
        )
        return found

    def send_labels(step, carry):
        label_copy(step).start()
        return carry

    lax.fori_loop(1, n_sector, send_labels, 0)
    load_psi.wait()
    load_left.wait()

    def contract(buffer, step):
        found = find(lambda w, s: target[w, s], shifted(me, step, 1, n_sector))
        for slot in range(CAP):
            item = jnp.maximum(found[slot], 0) // blocks
            value = jnp.dot(
                left[item], psi[item % blocks],
                precision=lax.Precision.HIGHEST, preferred_element_type=jnp.float32,
            )
            for chunk in range(CHUNKS):
                for t in range(n_term):
                    first = t * rows + chunk * part
                    buffer[chunk, step, slot, t * part:(t + 1) * part, :] = value[first:first + part]

    def contract_and_send(i, carry):
        step = n_sector - 1 - i
        contract(send, step)
        data_copy(0, step).start()
        return carry

    lax.fori_loop(0, n_sector - 1, contract_and_send, 0)

    def send_later(i, carry):
        step = n_sector - 1 - i
        for chunk in range(1, CHUNKS):
            data_copy(chunk, step).start()
        return carry

    lax.fori_loop(0, n_sector - 1, send_later, 0)
    contract(recv, 0)

    def keep(step, read):
        found = find(read, me)
        for slot in range(CAP):
            code = found[slot]
            item = jnp.maximum(code, 0) // blocks
            local = jnp.where(code >= 0, code % blocks, -1)
            held_items[step, slot] = item // blocks * blocks + jnp.maximum(local, 0)
            held_labels[step, slot] = local

    keep(0, lambda w, s: target[w, s])

    def labels_arrived(step, carry):
        label_copy(step).wait_recv()
        return carry

    def keep_arrived(step, carry):
        keep(step, lambda w, s: labels[step, w, s])
        return carry

    lax.fori_loop(1, n_sector, labels_arrived, 0)
    lax.fori_loop(1, n_sector, keep_arrived, 0)
    load_right.wait()
    partial[...] = jnp.zeros_like(partial)

    def multiply(chunk, step):
        values, owners = [], []
        for slot in range(CAP):
            values.append(jnp.dot(
                recv[chunk, step, slot], right[held_items[step, slot]],
                precision=lax.Precision.HIGHEST, preferred_element_type=jnp.float32,
            ))
            owners.append(held_labels[step, slot])
        for s in range(blocks):
            add = jnp.where(owners[0] == s, values[0], 0.0)
            for slot in range(1, CAP):
                add = add + jnp.where(owners[slot] == s, values[slot], 0.0)
            for t in range(n_term):
                partial[chunk, t, s] += add[t * part:(t + 1) * part]

    def term_copy(chunk, other):
        return pltpu.make_async_remote_copy(
            src_ref=partial.at[chunk, lax.rem(my_term + other, n_term)],
            dst_ref=from_term.at[chunk, other - 1],
            send_sem=term_send.at[chunk, other - 1],
            recv_sem=term_recv.at[chunk, other - 1],
            device_id={"term": lax.rem(my_term + other, n_term)},
            device_id_type=MESH,
        )

    for chunk in range(CHUNKS):
        multiply(chunk, 0)

        def arrived(i, carry, chunk=chunk):
            step = n_sector - 1 - i
            data_copy(chunk, step).wait_recv()
            multiply(chunk, step)
            return carry

        lax.fori_loop(0, n_sector - 1, arrived, 0)
        for other in range(1, n_term):
            term_copy(chunk, other).start()

    for chunk in range(CHUNKS):
        for other in range(1, n_term):
            term_copy(chunk, other).wait_recv()
        total = partial[chunk, my_term]
        for other in range(1, n_term):
            total = total + from_term[chunk, other - 1]
        out[:, chunk * part:(chunk + 1) * part, :] = total

    for chunk in range(CHUNKS):
        for other in range(1, n_term):
            term_copy(chunk, other).wait_send()

    def drain(step, carry):
        label_copy(step).wait_send()
        for chunk in range(CHUNKS):
            data_copy(chunk, step).wait_send()
        return carry

    lax.fori_loop(1, n_sector, drain, 0)


def on_device(n_sector, n_term, psi, left_env, right_env, target):
    blocks, width, _ = psi.shape
    terms = left_env.shape[0]
    items = terms * blocks
    rows = width // n_term
    part = rows // CHUNKS
    flops = 2 * 2 * items * width ** 3
    return pl.pallas_call(
        functools.partial(kernel, n_sector, n_term),
        out_shape=jax.ShapeDtypeStruct((blocks, rows, width), jnp.float32),
        in_specs=[pl.BlockSpec(memory_space=pltpu.SMEM)] + [pl.BlockSpec(memory_space=pl.ANY)] * 3,
        out_specs=pl.BlockSpec(memory_space=pltpu.VMEM),
        scratch_shapes=[
            pltpu.VMEM((blocks, width, width), jnp.float32),
            pltpu.VMEM((items, width, width), jnp.float32),
            pltpu.VMEM((items, width, width), jnp.float32),
            pltpu.VMEM((CHUNKS, n_sector, CAP, n_term * part, width), jnp.float32),
            pltpu.VMEM((CHUNKS, n_sector, CAP, n_term * part, width), jnp.float32),
            pltpu.VMEM((CHUNKS, n_term, blocks, part, width), jnp.float32),
            pltpu.VMEM((CHUNKS, max(n_term - 1, 1), blocks, part, width), jnp.float32),
            pltpu.SMEM((n_sector, terms, blocks), jnp.int32),
            pltpu.SMEM((n_sector, CAP), jnp.int32),
            pltpu.SMEM((n_sector, CAP), jnp.int32),
            pltpu.SemaphoreType.DMA((3,)),
            pltpu.SemaphoreType.DMA((n_sector,)),
            pltpu.SemaphoreType.DMA((n_sector,)),
            pltpu.SemaphoreType.DMA((CHUNKS, n_sector)),
            pltpu.SemaphoreType.DMA((CHUNKS, n_sector)),
            pltpu.SemaphoreType.DMA((CHUNKS, max(n_term - 1, 1))),
            pltpu.SemaphoreType.DMA((CHUNKS, max(n_term - 1, 1))),
        ],
        compiler_params=pltpu.CompilerParams(
            collective_id=0, has_side_effects=True, vmem_limit_bytes=48 * 1024 * 1024
        ),
        cost_estimate=pl.CostEstimate(
            flops=flops, bytes_accessed=(2 * items + 2 * blocks) * width * width * 4, transcendentals=0
        ),
    )(
        target, psi,
        left_env.reshape(items, width, width),
        right_env.reshape(items, width, width),
    )


def solution(mesh):
    in_specs = (
        P("sector", None, None),
        P("term", "sector", None, None),
        P("term", "sector", None, None),
        P("term", "sector"),
    )
    return jax.shard_map(
        functools.partial(on_device, mesh.shape["sector"], mesh.shape["term"]),
        mesh=mesh, in_specs=in_specs, out_specs=P("sector", "term", None), check_vma=False,
    )
```

```python
import functools

import jax
import jax.numpy as jnp
from jax import lax
from jax.experimental import pallas as pl
from jax.experimental.pallas import tpu as pltpu
from jax.sharding import PartitionSpec as P

CAP = 4
PARTS = (5, 2, 1)
MESH = pl.DeviceIdType.MESH


def row_parts(rows):
    units = rows // 8
    parts = PARTS if units == sum(PARTS) else (1,) * units
    starts = [8 * sum(parts[:i]) for i in range(len(parts))]
    return list(zip(starts, [8 * p for p in parts]))


def shifted(me, step, count):
    high = count // 4
    d_high, d_mid, d_low = step // 4, (step // 2) % 2, step % 2
    z, x, c = me // 4, (me // 2) % 2, me % 2
    z = lax.rem(z + d_high, high)
    x = lax.rem(x + d_mid, 2)
    c = lax.rem(c + d_low, 2)
    return (z * 2 + x) * 2 + c


def kernel(
    n_sector, n_term, target, psi_hbm, left_hbm, right_hbm, out,
    psi, left, right, send, recv, partial, from_term,
    labels, held_items, held_labels,
    load_sem, label_send, label_recv, data_send, data_recv, term_send, term_recv,
):
    terms, blocks = target.shape
    width = psi.shape[-1]
    rows = width // n_term
    parts = row_parts(rows)
    chunks = len(parts)
    me = lax.axis_index("sector")
    my_term = lax.axis_index("term")

    load_psi = pltpu.make_async_copy(psi_hbm, psi, load_sem.at[0])
    load_left = pltpu.make_async_copy(left_hbm, left, load_sem.at[1])
    load_right = pltpu.make_async_copy(right_hbm, right, load_sem.at[2])
    load_psi.start()
    load_left.start()
    load_right.start()

    barrier = pltpu.get_barrier_semaphore()

    def greet(step, carry):
        peer = shifted(me, step, n_sector)
        pl.semaphore_signal(barrier, inc=1, device_id={"sector": peer}, device_id_type=MESH)
        return carry

    lax.fori_loop(1, n_sector, greet, 0)
    for other in range(1, n_term):
        pl.semaphore_signal(
            barrier, inc=1, device_id={"term": lax.rem(my_term + other, n_term)}, device_id_type=MESH
        )
    pl.semaphore_wait(barrier, n_sector + n_term - 2)

    def label_copy(step):
        return pltpu.make_async_remote_copy(
            src_ref=target,
            dst_ref=labels.at[step],
            send_sem=label_send.at[step],
            recv_sem=label_recv.at[step],
            device_id={"sector": shifted(me, step, n_sector)},
            device_id_type=MESH,
        )

    def data_copy(chunk, step):
        return pltpu.make_async_remote_copy(
            src_ref=send[chunk].at[step],
            dst_ref=recv[chunk].at[step],
            send_sem=data_send.at[chunk, step],
            recv_sem=data_recv.at[chunk, step],
            device_id={"sector": shifted(me, step, n_sector)},
            device_id_type=MESH,
        )

    base = 2 * terms * blocks
    assert terms * blocks < base and base ** CAP < 2 ** 31

    def find(read, owner):
        low = owner * blocks
        high = low + blocks
        found = jnp.int32(0)
        for w in range(terms):

            def scan(s, found, w=w):
                target_block = read(w, s)
                hit = (target_block >= low) & (target_block < high)
                return jnp.where(hit, found * base + (w * blocks + s + 1), found)

            found = lax.fori_loop(0, blocks, scan, found, unroll=True)
        digits = []
        for _ in range(CAP):
            digits.append(lax.rem(found, base))
            found = lax.div(found, base)
        return digits

    def order(i):
        return 1 + i

    def send_labels(step, carry):
        label_copy(step).start()
        return carry

    lax.fori_loop(1, n_sector, send_labels, 0)
    load_psi.wait()
    load_left.wait()

    def contract(buffer, step):
        found = find(lambda w, s: target[w, s], shifted(me, step, n_sector))
        for slot in range(CAP):
            item = jnp.maximum(found[slot] - 1, 0)
            value = jnp.dot(
                left[item], psi[lax.rem(item, blocks)],
                precision=lax.Precision.HIGHEST, preferred_element_type=jnp.float32,
            )
            for chunk, (start, part) in enumerate(parts):
                for t in range(n_term):
                    first = t * rows + start
                    buffer[chunk][step, slot, t * part:(t + 1) * part, :] = value[first:first + part]

    def contract_and_send(i, carry):
        step = order(i)
        contract(send, step)
        data_copy(0, step).start()
        return carry

    lax.fori_loop(0, n_sector - 1, contract_and_send, 0)

    for chunk in range(1, chunks):

        def send_later(i, carry, chunk=chunk):
            data_copy(chunk, order(i)).start()
            return carry

        lax.fori_loop(0, n_sector - 1, send_later, 0)
    contract(recv, 0)

    def keep(step, read):
        found = find(read, me)
        for slot in range(CAP):
            item = jnp.maximum(found[slot] - 1, 0)
            local = read(lax.div(item, blocks), lax.rem(item, blocks)) - me * blocks
            held_items[step, slot] = lax.div(item, blocks) * blocks + jnp.clip(local, 0, blocks - 1)
            held_labels[step, slot] = jnp.where(found[slot] > 0, local, -1)

    keep(0, lambda w, s: target[w, s])

    def labels_arrived(step, carry):
        label_copy(step).wait_recv()
        return carry

    def keep_arrived(step, carry):
        keep(step, lambda w, s: labels[step, w, s])
        return carry

    lax.fori_loop(1, n_sector, labels_arrived, 0)
    lax.fori_loop(1, n_sector, keep_arrived, 0)
    load_right.wait()
    for ref in partial:
        ref[...] = jnp.zeros_like(ref)

    def multiply(chunk, step):
        part = parts[chunk][1]
        values, owners = [], []
        for slot in range(CAP):
            values.append(jnp.dot(
                recv[chunk][step, slot], right[held_items[step, slot]],
                precision=lax.Precision.HIGHEST, preferred_element_type=jnp.float32,
            ))
            owners.append(held_labels[step, slot])
        for s in range(blocks):
            add = jnp.where(owners[0] == s, values[0], 0.0)
            for slot in range(1, CAP):
                add = add + jnp.where(owners[slot] == s, values[slot], 0.0)
            for t in range(n_term):
                partial[chunk][t, s] += add[t * part:(t + 1) * part]

    def term_copy(chunk, other):
        return pltpu.make_async_remote_copy(
            src_ref=partial[chunk].at[lax.rem(my_term + other, n_term)],
            dst_ref=from_term[chunk].at[other - 1],
            send_sem=term_send.at[chunk, other - 1],
            recv_sem=term_recv.at[chunk, other - 1],
            device_id={"term": lax.rem(my_term + other, n_term)},
            device_id_type=MESH,
        )

    for chunk in range(chunks):
        multiply(chunk, 0)

        def arrived(i, carry, chunk=chunk):
            step = order(i)
            data_copy(chunk, step).wait_recv()
            multiply(chunk, step)
            return carry

        lax.fori_loop(0, n_sector - 1, arrived, 0)
        for other in range(1, n_term):
            term_copy(chunk, other).start()

    for chunk, (start, part) in enumerate(parts):
        for other in range(1, n_term):
            term_copy(chunk, other).wait_recv()
        total = partial[chunk][my_term]
        for other in range(1, n_term):
            total = total + from_term[chunk][other - 1]
        out[:, start:start + part, :] = total

    for chunk in range(chunks):
        for other in range(1, n_term):
            term_copy(chunk, other).wait_send()

    def drain(step, carry):
        label_copy(step).wait_send()
        for chunk in range(chunks):
            data_copy(chunk, step).wait_send()
        return carry

    lax.fori_loop(1, n_sector, drain, 0)


def on_device(n_sector, n_term, psi, left_env, right_env, target):
    blocks, width, _ = psi.shape
    terms = left_env.shape[0]
    items = terms * blocks
    rows = width // n_term
    parts = [part for _, part in row_parts(rows)]
    chunks = len(parts)
    flops = 2 * 2 * items * width ** 3
    return pl.pallas_call(
        functools.partial(kernel, n_sector, n_term),
        out_shape=jax.ShapeDtypeStruct((blocks, rows, width), jnp.float32),
        in_specs=[pl.BlockSpec(memory_space=pltpu.SMEM)] + [pl.BlockSpec(memory_space=pl.ANY)] * 3,
        out_specs=pl.BlockSpec(memory_space=pltpu.VMEM),
        scratch_shapes=[
            pltpu.VMEM((blocks, width, width), jnp.float32),
            pltpu.VMEM((items, width, width), jnp.float32),
            pltpu.VMEM((items, width, width), jnp.float32),
            [pltpu.VMEM((n_sector, CAP, n_term * part, width), jnp.float32) for part in parts],
            [pltpu.VMEM((n_sector, CAP, n_term * part, width), jnp.float32) for part in parts],
            [pltpu.VMEM((n_term, blocks, part, width), jnp.float32) for part in parts],
            [pltpu.VMEM((max(n_term - 1, 1), blocks, part, width), jnp.float32) for part in parts],
            pltpu.SMEM((n_sector, terms, blocks), jnp.int32),
            pltpu.SMEM((n_sector, CAP), jnp.int32),
            pltpu.SMEM((n_sector, CAP), jnp.int32),
            pltpu.SemaphoreType.DMA((3,)),
            pltpu.SemaphoreType.DMA((n_sector,)),
            pltpu.SemaphoreType.DMA((n_sector,)),
            pltpu.SemaphoreType.DMA((chunks, n_sector)),
            pltpu.SemaphoreType.DMA((chunks, n_sector)),
            pltpu.SemaphoreType.DMA((chunks, max(n_term - 1, 1))),
            pltpu.SemaphoreType.DMA((chunks, max(n_term - 1, 1))),
        ],
        compiler_params=pltpu.CompilerParams(
            collective_id=0, has_side_effects=True, vmem_limit_bytes=48 * 1024 * 1024
        ),
        cost_estimate=pl.CostEstimate(
            flops=flops, bytes_accessed=(2 * items + 2 * blocks) * width * width * 4, transcendentals=0
        ),
    )(
        target, psi,
        left_env.reshape(items, width, width),
        right_env.reshape(items, width, width),
    )


def solution(mesh):
    in_specs = (
        P("sector", None, None),
        P("term", "sector", None, None),
        P("term", "sector", None, None),
        P("term", "sector"),
    )
    return jax.shard_map(
        functools.partial(on_device, mesh.shape["sector"], mesh.shape["term"]),
        mesh=mesh, in_specs=in_specs, out_specs=P("sector", "term", None), check_vma=False,
    )
```

```python
import functools

import jax
import jax.numpy as jnp
from jax import lax
from jax.experimental import pallas as pl
from jax.experimental.pallas import tpu as pltpu
from jax.sharding import PartitionSpec as P

CAP = 4
PARTS = (5, 2, 1)
MESH = pl.DeviceIdType.MESH


def row_parts(rows):
    units = rows // 8
    parts = PARTS if units == sum(PARTS) else (1,) * units
    starts = [8 * sum(parts[:i]) for i in range(len(parts))]
    return list(zip(starts, [8 * p for p in parts]))


def shifted(me, step, count):
    high = count // 4
    d_high, d_mid, d_low = step // 4, (step // 2) % 2, step % 2
    z, x, c = me // 4, (me // 2) % 2, me % 2
    z = lax.rem(z + d_high, high)
    x = lax.rem(x + d_mid, 2)
    c = lax.rem(c + d_low, 2)
    return (z * 2 + x) * 2 + c


def kernel(
    n_sector, n_term, target, psi_hbm, left_hbm, right_hbm, out,
    psi, left, right, send, recv, partial, from_term,
    labels, held_items, held_labels,
    load_sem, label_send, label_recv, data_send, data_recv, term_send, term_recv,
):
    terms, blocks = target.shape
    width = psi.shape[-1]
    rows = width // n_term
    parts = row_parts(rows)
    chunks = len(parts)
    me = lax.axis_index("sector")
    my_term = lax.axis_index("term")

    load_psi = pltpu.make_async_copy(psi_hbm, psi, load_sem.at[0])
    load_left = pltpu.make_async_copy(left_hbm, left, load_sem.at[1])
    load_right = pltpu.make_async_copy(right_hbm, right, load_sem.at[2])
    load_psi.start()
    load_left.start()
    load_right.start()

    barrier = pltpu.get_barrier_semaphore()

    def greet(step, carry):
        peer = shifted(me, step, n_sector)
        pl.semaphore_signal(barrier, inc=1, device_id={"sector": peer}, device_id_type=MESH)
        return carry

    lax.fori_loop(1, n_sector, greet, 0)
    for other in range(1, n_term):
        pl.semaphore_signal(
            barrier, inc=1, device_id={"term": lax.rem(my_term + other, n_term)}, device_id_type=MESH
        )
    pl.semaphore_wait(barrier, n_sector + n_term - 2)

    def label_copy(step):
        return pltpu.make_async_remote_copy(
            src_ref=target,
            dst_ref=labels.at[step],
            send_sem=label_send.at[step],
            recv_sem=label_recv.at[step],
            device_id={"sector": shifted(me, step, n_sector)},
            device_id_type=MESH,
        )

    def data_copy(chunk, step):
        return pltpu.make_async_remote_copy(
            src_ref=send[chunk].at[step],
            dst_ref=recv[chunk].at[step],
            send_sem=data_send.at[chunk, step],
            recv_sem=data_recv.at[chunk, step],
            device_id={"sector": shifted(me, step, n_sector)},
            device_id_type=MESH,
        )

    base = 2 * terms * blocks
    assert terms * blocks < base and base ** CAP < 2 ** 31

    def find(read, owner):
        low = owner * blocks
        high = low + blocks
        found = jnp.int32(0)
        for w in range(terms):

            def scan(s, found, w=w):
                target_block = read(w, s)
                hit = (target_block >= low) & (target_block < high)
                return jnp.where(hit, found * base + (w * blocks + s + 1), found)

            found = lax.fori_loop(0, blocks, scan, found, unroll=True)
        digits = []
        for _ in range(CAP):
            digits.append(lax.rem(found, base))
            found = lax.div(found, base)
        return digits

    def order(i):
        return 1 + i

    def send_labels(step, carry):
        label_copy(step).start()
        return carry

    lax.fori_loop(1, n_sector, send_labels, 0)
    load_psi.wait()
    load_left.wait()

    def contract(buffer, step):
        found = find(lambda w, s: target[w, s], shifted(me, step, n_sector))
        for slot in range(CAP):
            item = jnp.maximum(found[slot] - 1, 0)
            value = jnp.dot(
                left[item], psi[lax.rem(item, blocks)],
                precision=lax.Precision.HIGHEST, preferred_element_type=jnp.float32,
            )
            for chunk, (start, part) in enumerate(parts):
                for t in range(n_term):
                    first = t * rows + start
                    buffer[chunk][step, slot, t * part:(t + 1) * part, :] = value[first:first + part]

    def contract_and_send(i, carry):
        step = order(i)
        contract(send, step)
        data_copy(0, step).start()
        return carry

    lax.fori_loop(0, n_sector - 1, contract_and_send, 0)

    for chunk in range(1, chunks):

        def send_later(i, carry, chunk=chunk):
            data_copy(chunk, order(i)).start()
            return carry

        lax.fori_loop(0, n_sector - 1, send_later, 0)
    contract(recv, 0)

    def keep(step, read):
        found = find(read, me)
        for slot in range(CAP):
            item = jnp.maximum(found[slot] - 1, 0)
            local = read(lax.div(item, blocks), lax.rem(item, blocks)) - me * blocks
            held_items[step, slot] = lax.div(item, blocks) * blocks + jnp.clip(local, 0, blocks - 1)
            held_labels[step, slot] = jnp.where(found[slot] > 0, local, -1)

    keep(0, lambda w, s: target[w, s])

    def labels_arrived(step, carry):
        label_copy(step).wait_recv()
        return carry

    def keep_arrived(step, carry):
        keep(step, lambda w, s: labels[step, w, s])
        return carry

    lax.fori_loop(1, n_sector, labels_arrived, 0)
    lax.fori_loop(1, n_sector, keep_arrived, 0)
    load_right.wait()
    for ref in partial:
        ref[...] = jnp.zeros_like(ref)

    def multiply(chunk, step):
        part = parts[chunk][1]
        values, owners = [], []
        for slot in range(CAP):
            values.append(jnp.dot(
                recv[chunk][step, slot], right[held_items[step, slot]],
                precision=lax.Precision.HIGHEST, preferred_element_type=jnp.float32,
            ))
            owners.append(held_labels[step, slot])
        for s in range(blocks):
            add = jnp.where(owners[0] == s, values[0], 0.0)
            for slot in range(1, CAP):
                add = add + jnp.where(owners[slot] == s, values[slot], 0.0)
            for t in range(n_term):
                partial[chunk][t, s] += add[t * part:(t + 1) * part]

    def term_copy(chunk, other):
        return pltpu.make_async_remote_copy(
            src_ref=partial[chunk].at[lax.rem(my_term + other, n_term)],
            dst_ref=from_term[chunk].at[other - 1],
            send_sem=term_send.at[chunk, other - 1],
            recv_sem=term_recv.at[chunk, other - 1],
            device_id={"term": lax.rem(my_term + other, n_term)},
            device_id_type=MESH,
        )

    for chunk in range(chunks):
        multiply(chunk, 0)

        def arrived(i, carry, chunk=chunk):
            step = order(i)
            data_copy(chunk, step).wait_recv()
            multiply(chunk, step)
            return carry

        lax.fori_loop(0, n_sector - 1, arrived, 0)
        for other in range(1, n_term):
            term_copy(chunk, other).start()

    for chunk, (start, part) in enumerate(parts):
        for other in range(1, n_term):
            term_copy(chunk, other).wait_recv()
        total = partial[chunk][my_term]
        for other in range(1, n_term):
            total = total + from_term[chunk][other - 1]
        out[:, start:start + part, :] = total

    for chunk in range(chunks):
        for other in range(1, n_term):
            term_copy(chunk, other).wait_send()

    def drain(step, carry):
        label_copy(step).wait_send()
        for chunk in range(chunks):
            data_copy(chunk, step).wait_send()
        return carry

    lax.fori_loop(1, n_sector, drain, 0)


def on_device(n_sector, n_term, psi, left_env, right_env, target):
    blocks, width, _ = psi.shape
    terms = left_env.shape[0]
    items = terms * blocks
    rows = width // n_term
    parts = [part for _, part in row_parts(rows)]
    chunks = len(parts)
    flops = 2 * 2 * items * width ** 3
    return pl.pallas_call(
        functools.partial(kernel, n_sector, n_term),
        out_shape=jax.ShapeDtypeStruct((blocks, rows, width), jnp.float32),
        in_specs=[pl.BlockSpec(memory_space=pltpu.SMEM)] + [pl.BlockSpec(memory_space=pl.ANY)] * 3,
        out_specs=pl.BlockSpec(memory_space=pltpu.VMEM),
        scratch_shapes=[
            pltpu.VMEM((blocks, width, width), jnp.float32),
            pltpu.VMEM((items, width, width), jnp.float32),
            pltpu.VMEM((items, width, width), jnp.float32),
            [pltpu.VMEM((n_sector, CAP, n_term * part, width), jnp.float32) for part in parts],
            [pltpu.VMEM((n_sector, CAP, n_term * part, width), jnp.float32) for part in parts],
            [pltpu.VMEM((n_term, blocks, part, width), jnp.float32) for part in parts],
            [pltpu.VMEM((max(n_term - 1, 1), blocks, part, width), jnp.float32) for part in parts],
            pltpu.SMEM((n_sector, terms, blocks), jnp.int32),
            pltpu.SMEM((n_sector, CAP), jnp.int32),
            pltpu.SMEM((n_sector, CAP), jnp.int32),
            pltpu.SemaphoreType.DMA((3,)),
            pltpu.SemaphoreType.DMA((n_sector,)),
            pltpu.SemaphoreType.DMA((n_sector,)),
            pltpu.SemaphoreType.DMA((chunks, n_sector)),
            pltpu.SemaphoreType.DMA((chunks, n_sector)),
            pltpu.SemaphoreType.DMA((chunks, max(n_term - 1, 1))),
            pltpu.SemaphoreType.DMA((chunks, max(n_term - 1, 1))),
        ],
        compiler_params=pltpu.CompilerParams(
            collective_id=0, has_side_effects=True, vmem_limit_bytes=56 * 1024 * 1024
        ),
        cost_estimate=pl.CostEstimate(
            flops=flops, bytes_accessed=(2 * items + 2 * blocks) * width * width * 4, transcendentals=0
        ),
    )(
        target, psi,
        left_env.reshape(items, width, width),
        right_env.reshape(items, width, width),
    )


def solution(mesh):
    in_specs = (
        P("sector", None, None),
        P("term", "sector", None, None),
        P("term", "sector", None, None),
        P("term", "sector"),
    )
    return jax.shard_map(
        functools.partial(on_device, mesh.shape["sector"], mesh.shape["term"]),
        mesh=mesh, in_specs=in_specs, out_specs=P("sector", "term", None), check_vma=False,
    )
```
